128 devices in a mesh: shard: 16 (over x, y), sub: 8 (over z, core).
Axes of the slice: x: 4, y: 4, z: 4, core: 2. Of those that a mesh axis runs over, the one named last changes fastest.
Arguments:
- embeddings: bfloat16 [98304, 256], P(('shard', 'sub')), may hold values from -16 to 16
- subspace: float32 [98304, 128], P(('shard', 'sub')), may hold values from -6 to 6
- pair_slots: int32 [16, 8, 8, 2], P('shard', 'sub'), may hold values from 0 to 15, as said below
- pair_count: int32 [16, 8], P('shard', 'sub'), may hold values from 2 to 8, as said below
Outputs:
- spectral_basis: float32 [98304, 128], P(('shard', 'sub'))
The draws below stay inside these ranges and needn't reach their ends.
Inputs may be any that keep to these rules, and one draw needn't show every extreme that they name: `pair_slots`: each owner's first pair_count slots name distinct pairs, never its own block with itself; later slots hold valid positions but are not used. Row positions are below 8, column positions below 16. `pair_count`: live pair slots of one device; some device has exactly 8.
All inputs are finite; a program needn't handle non-finite values.
Results may differ from the reference program's by a relative error of at most 0.012.
The reference program's roundings to bfloat16 on the way (of `normed`, `basis` and `tile`) count: a program that leaves them out, or rounds other values in their place, can miss the bound.
Values may be sent and summed in bfloat16 or wider, within the bound.
No kernel may reach another device: no remote copies, remote signals or barrier semaphores. Data moves between devices by JAX's collectives and lax.ppermute only.
A program may use at most 64 MiB of HBM per device.

```python
import math
import jax
import jax.numpy as jnp
from jax import lax

FEAT = 256
RANK = 128
BLOCK = 768
CAP = 8
ITERS = 2
SHARDS = 16
SUBS = 8
BLOCKS = 128
ROWS = 98304


def draw_embeddings(key, part):
    key = jax.random.fold_in(key, 7)
    pick_key, centre_key, noise_key, spread_key = jax.random.split(key, 4)
    groups = BLOCK
    scores = jax.random.randint(pick_key, (BLOCKS, BLOCK), 0, 65536, dtype=jnp.int32) * BLOCK + jnp.arange(BLOCK, dtype=jnp.int32)[None, :]
    labels = jnp.argsort(scores, axis=-1).astype(jnp.int32).reshape(ROWS)
    centres = jax.random.normal(centre_key, (groups, FEAT), jnp.float32)
    spread = jnp.exp(jax.random.uniform(spread_key, (ROWS, 1), jnp.float32, math.log(0.1), math.log(0.3)))
    noise_part = jax.random.normal(noise_key, (ROWS, FEAT), jnp.float32)
    values = jnp.take(centres, labels, axis=0) + spread * noise_part
    return jnp.clip(values, -16.0, 16.0).astype(jnp.bfloat16)


def draw_pair_slots(key, part):
    key = jax.random.fold_in(key, 11)
    combos = SUBS * SHARDS
    shard_pos = jnp.arange(SHARDS, dtype=jnp.int32)[:, None, None]
    sub_pos = jnp.arange(SUBS, dtype=jnp.int32)[None, :, None]
    combo = jnp.arange(combos, dtype=jnp.int32)[None, None, :]
    row_pos = combo // SHARDS
    col_pos = combo % SHARDS
    banned = (row_pos == sub_pos) & (col_pos == shard_pos)
    scores = jax.random.randint(key, (SHARDS, SUBS, combos), 0, 65536, dtype=jnp.int32) * combos + combo
    scores = jnp.where(banned, 65536 * combos + combo, scores)
    order = jnp.argsort(scores, axis=-1, stable=True)[:, :, :CAP].astype(jnp.int32)
    return jnp.stack([order // SHARDS, order % SHARDS], axis=-1).astype(jnp.int32)


def draw_pair_count(key, part):
    key = jax.random.fold_in(key, 23)
    first, second, third = jax.random.split(key, 3)
    base = jax.random.randint(first, (SHARDS, SUBS), max(1, CAP // 4), CAP // 2 + 1, dtype=jnp.int32)
    heavy = jax.random.randint(second, (SHARDS, SUBS), 0, 8, dtype=jnp.int32) == 0
    counts = jnp.where(heavy, CAP, base)
    forced = jax.random.randint(third, (), 0, SHARDS * SUBS, dtype=jnp.int32)
    flat_pos = jnp.arange(SHARDS * SUBS, dtype=jnp.int32).reshape(SHARDS, SUBS)
    return jnp.where(flat_pos == forced, CAP, counts).astype(jnp.int32)


def block_levels(stream_key, shape, shards, least, high):
    loudness = 1.0
    for axis_at, parts in shards:
        draws = jax.random.uniform(jax.random.fold_in(jax.random.fold_in(stream_key, 6), axis_at), (parts,), jnp.float32, least / len(shards), high / len(shards))
        loudness = loudness * jnp.repeat(jnp.exp(draws), shape[axis_at] // parts).reshape((-1,) + (1,) * (len(shape) - 1 - axis_at))
    return loudness


def scatter_about(own_key, dims, deviation, bound, shards=(), kind=jnp.bfloat16):
    loudness = block_levels(own_key, dims, shards, -0.22, 0.18) if shards else 1.0
    result = jax.random.normal(own_key, dims, jnp.float32) * deviation * loudness
    return jnp.minimum(jnp.maximum(result, -bound), bound).astype(kind)


def setup_inputs(seed: int = 0) -> dict:
    splits = jax.random.split(jax.random.key(seed), 5)
    embeddings = draw_embeddings(jax.random.fold_in(splits[4], 71), 0)
    subspace = scatter_about(splits[1], (ROWS, RANK), 1.0, 6.0, ((0, 128),), jnp.float32)
    pair_slots = draw_pair_slots(jax.random.fold_in(splits[4], 71), 0)
    pair_count = draw_pair_count(jax.random.fold_in(splits[4], 71), 0)
    return {"embeddings": embeddings, "subspace": subspace, "pair_slots": pair_slots, "pair_count": pair_count}


sharpness = 10.0

def normalize(embeddings):
    values = embeddings.astype(jnp.float32)
    scale = lax.rsqrt(lax.optimization_barrier(jnp.mean(values * values, axis=-1, keepdims=True)) + 1e-06) / jnp.sqrt(jnp.float32(values.shape[-1]))
    return (values * scale).astype(jnp.bfloat16)

def kernel_tile(left, right):
    sims = lax.dot_general(left.astype(jnp.float32), right.astype(jnp.float32), (((1,), (1,)), ((), ())), preferred_element_type=jnp.float32)
    return jnp.exp(sharpness * (sims - 1.0)).astype(jnp.bfloat16)

def column_product(tile, basis):
    return lax.dot_general(tile.astype(jnp.float32), basis.astype(jnp.float32), (((0,), (0,)), ((), ())), preferred_element_type=jnp.float32)

def reference(embeddings, subspace, pair_slots, pair_count):
    normed = normalize(embeddings).reshape(BLOCKS, BLOCK, FEAT)
    slots_flat = pair_slots.reshape(BLOCKS, CAP, 2)
    counts_flat = pair_count.reshape(BLOCKS)
    current = subspace
    for iteration in range(ITERS):
        basis = current.astype(jnp.bfloat16).reshape(BLOCKS, BLOCK, RANK)

        def own_term(pieces):
            return jnp.dot(kernel_tile(pieces[0], pieces[0]).astype(jnp.float32), pieces[1].astype(jnp.float32), preferred_element_type=jnp.float32)
        own = lax.map(own_term, (normed, basis))

        def device_step(total, inputs):
            device, slots, count = inputs
            shard_pos = device // SUBS
            sub_pos = device % SUBS

            def add_pair(slot_pos, sums):

                def apply(sums_in):
                    row_acc, col_acc = sums_in
                    pick_row = slots[slot_pos, 0]
                    pick_col = slots[slot_pos, 1]
                    row_block = (shard_pos * SUBS + pick_row).astype(jnp.int32)
                    col_block = (pick_col * SUBS + sub_pos).astype(jnp.int32)
                    left = lax.dynamic_index_in_dim(normed, row_block, 0, keepdims=False)
                    right = lax.dynamic_index_in_dim(normed, col_block, 0, keepdims=False)
                    tile = kernel_tile(left, right)
                    row_new = jnp.dot(tile.astype(jnp.float32), lax.dynamic_index_in_dim(basis, col_block, 0, keepdims=False).astype(jnp.float32), preferred_element_type=jnp.float32)
                    col_new = column_product(tile, lax.dynamic_index_in_dim(basis, row_block, 0, keepdims=False))
                    row_acc = lax.dynamic_update_index_in_dim(row_acc, lax.dynamic_index_in_dim(row_acc, pick_row, 0, keepdims=False) + row_new, pick_row, 0)
                    col_acc = lax.dynamic_update_index_in_dim(col_acc, lax.dynamic_index_in_dim(col_acc, pick_col, 0, keepdims=False) + col_new, pick_col, 0)
                    return (row_acc, col_acc)

                def keep_sums(sums_in):
                    return sums_in
                return lax.cond(slot_pos < count, apply, keep_sums, sums)
            start = (jnp.zeros((SUBS, BLOCK, RANK), jnp.float32), jnp.zeros((SHARDS, BLOCK, RANK), jnp.float32))
            row_acc, col_acc = lax.fori_loop(0, CAP, add_pair, start)
            row_round = lax.optimization_barrier(row_acc.astype(jnp.bfloat16)).astype(jnp.float32)
            col_round = lax.optimization_barrier(col_acc.astype(jnp.bfloat16)).astype(jnp.float32)
            row_targets = shard_pos * SUBS + jnp.arange(SUBS, dtype=jnp.int32)
            col_targets = jnp.arange(SHARDS, dtype=jnp.int32) * SUBS + sub_pos
            total = total.at[row_targets].add(row_round)
            total = total.at[col_targets].add(col_round)
            return (total, None)
        total, unused = lax.scan(device_step, own, (jnp.arange(BLOCKS, dtype=jnp.int32), slots_flat, counts_flat))
        image = total.reshape(ROWS, RANK)
        gram = jnp.dot(image.T.astype(jnp.float32), image.astype(jnp.float32), precision=lax.Precision.HIGHEST, preferred_element_type=jnp.float32) / ROWS
        factor = jnp.linalg.cholesky(gram)
        current = jax.scipy.linalg.solve_triangular(factor, image.T, lower=True).T
    return current
```

```python
import functools

import jax
import jax.numpy as jnp
from jax import lax
from jax.experimental import pallas as pl
from jax.experimental.pallas import tpu as pltpu
from jax.sharding import PartitionSpec as P

ITERS = 2
SIDE = 4

sharpness = 10.0


def normalize(embeddings):
    values = embeddings.astype(jnp.float32)
    scale = lax.rsqrt(jnp.mean(values * values, axis=-1, keepdims=True) + 1e-06) / jnp.sqrt(
        jnp.float32(values.shape[-1])
    )
    return (values * scale).astype(jnp.bfloat16)


def move_x(array, step):
    pairs = [(x * SIDE + y, (x + step) % SIDE * SIDE + y) for x in range(SIDE) for y in range(SIDE)]
    return lax.ppermute(array, "shard", pairs)


def move_y(array, step):
    pairs = [(x * SIDE + y, x * SIDE + (y + step) % SIDE) for x in range(SIDE) for y in range(SIDE)]
    return lax.ppermute(array, "shard", pairs)


def move_z(array, step):
    pairs = [(z * 2 + c, (z + step) % SIDE * 2 + c) for z in range(SIDE) for c in range(2)]
    return lax.ppermute(array, "sub", pairs)


def swap_core(array):
    return lax.ppermute(array, "sub", [(z * 2 + c, z * 2 + 1 - c) for z in range(SIDE) for c in range(2)])


def total(*arrays):
    out = arrays[0].astype(jnp.float32)
    for array in arrays[1:]:
        out = out + array.astype(jnp.float32)
    return out


def gather_stack(move, array):
    return jnp.stack([array, move(array, 1), move(array, 2), move(array, 3)])


def gather_ring(move, stack):
    ahead, back = move(stack, 1), move(stack, 3)
    return [stack, ahead, back, move(ahead[:2], 1), move(back[2:], 3)]


def gather_cols(block):
    half = block.shape[0] // 2
    one = gather_stack(move_y, block[:half])
    two = gather_stack(move_x, block[half:])
    return gather_ring(move_x, one), gather_ring(move_y, two)


def scatter_ring(move, parts):
    far_ahead, far_back = move(parts[2][:2], 1), move(parts[2][2:], 3)
    ahead = jnp.concatenate([total(parts[1][:2], far_ahead).astype(jnp.bfloat16), parts[1][2:]])
    back = jnp.concatenate([parts[3][:2], total(parts[3][2:], far_back).astype(jnp.bfloat16)])
    return total(parts[0], move(ahead, 1), move(back, 3)).astype(jnp.bfloat16)


def scatter_direct(move, stack):
    return total(stack[0], *[move(stack[d], d) for d in (1, 2, 3)])


def scatter_cols(one, two):
    one = scatter_direct(move_y, scatter_ring(move_x, one))
    two = scatter_direct(move_x, scatter_ring(move_y, two))
    return jnp.concatenate([one, two])


def sum_everywhere(gram):
    gram = gram + swap_core(gram)
    for move in (move_z, move_y, move_x):
        gram = gram + move(gram, 1) + move(gram, 2) + move(gram, 3)
    return gram


NEAR = 5


def pairs_kernel(first, *refs):
    refs = list(refs)

    def take(n):
        out = refs[:n]
        del refs[:n]
        return out

    slots, own_in, rows_in = take(3)
    cols_one, cols_two = take(NEAR), take(NEAR)
    (tiles_in,) = (None,) if first else take(1)
    own_out, row_out = take(2)
    one_out, two_out = take(SIDE), take(SIDE)
    (tiles_out,) = take(1) if first else (None,)
    row_buf, col_buf, tile_buf, row_acc, col_acc, in_sem, tile_sem = refs

    block, rank = own_out.shape
    half = block // 2
    feat = row_buf.shape[-1] - rank if first else 0
    count, shard = slots[8, 0], slots[8, 1]
    my_x, my_y = shard // SIDE, lax.rem(shard, SIDE)

    def near(step, other):
        which = jnp.where(step < 2, step, jnp.where(step == 3, 2, jnp.where(other < 2, 3, 4)))
        return which, jnp.where((step == 2) & (other >= 2), other - 2, other)

    def copies(j, at):
        col = slots[j, 1]
        step_x = (my_x - col // SIDE + SIDE) & 3
        step_y = (my_y - lax.rem(col, SIDE) + SIDE) & 3
        fixed = [pltpu.make_async_copy(rows_in.at[slots[j, 0]], row_buf.at[at], in_sem.at[at, 0])]
        if not first:
            fixed.append(pltpu.make_async_copy(tiles_in.at[j], tile_buf.at[at], in_sem.at[at, 3]))
        picks = []
        for n, (stacks, (which, place)) in enumerate(
            ((cols_one, near(step_x, step_y)), (cols_two, near(step_y, step_x)))
        ):
            target = col_buf.at[at, pl.ds(n * half, half)]
            picks.append(
                [
                    (which == m, pltpu.make_async_copy(stack.at[place], target, in_sem.at[at, 1 + n]))
                    for m, stack in enumerate(stacks)
                ]
            )
        return fixed, picks

    def start(j, at):
        fixed, picks = copies(j, at)
        for copy in fixed:
            copy.start()
        for options in picks:
            for live, copy in options:
                pl.when(live)(copy.start)

    def finish(j, at):
        fixed, picks = copies(j, at)
        for copy in fixed:
            copy.wait()
        for options in picks:
            for live, copy in options:
                pl.when(live)(copy.wait)

    def tile_copy(j, at):
        return pltpu.make_async_copy(tile_buf.at[at], tiles_out.at[j], tile_sem.at[at])

    def fill_tile(left, right, at):
        for lo in range(0, block, 256):
            sims = lax.dot_general(
                left[pl.ds(lo, 256), :feat],
                right[:, :feat],
                (((1,), (1,)), ((), ())),
                preferred_element_type=jnp.float32,
            )
            tile_buf[at, pl.ds(lo, 256), :] = jnp.exp(sharpness * (sims - 1.0)).astype(jnp.bfloat16)

    start(0, 0)
    row_acc[...] = jnp.zeros_like(row_acc)
    col_acc[...] = jnp.zeros_like(col_acc)

    if first:
        fill_tile(own_in, own_in, 1)
        tile_copy(8, 1).start()
    else:
        own_tile = pltpu.make_async_copy(tiles_in.at[8], tile_buf.at[1], tile_sem.at[1])
        own_tile.start()
        own_tile.wait()
    own_out[...] = jnp.dot(tile_buf[1], own_in[:, feat:], preferred_element_type=jnp.float32)
    if first:
        tile_copy(8, 1).wait()

    @pl.loop(0, count)
    def _(j):
        at = lax.rem(j, 2)

        @pl.when(j + 1 < count)
        def _():
            start(j + 1, 1 - at)

        finish(j, at)
        if first:

            @pl.when(j >= 2)
            def _():
                tile_copy(j - 2, at).wait()

            fill_tile(row_buf.at[at], col_buf.at[at], at)
            tile_copy(j, at).start()
        row, col = slots[j, 0], slots[j, 1]
        row_acc[row] += jnp.dot(tile_buf[at], col_buf[at, :, feat:], preferred_element_type=jnp.float32)
        col_acc[col] += lax.dot_general(
            tile_buf[at],
            row_buf[at, :, feat:],
            (((0,), (0,)), ((), ())),
            preferred_element_type=jnp.float32,
        )

    if first:
        tile_copy(count - 1, lax.rem(count - 1, 2)).wait()

        @pl.when(count >= 2)
        def _():
            tile_copy(count - 2, lax.rem(count, 2)).wait()

    row_out[...] = row_acc[...].astype(jnp.bfloat16)
    for dx in range(SIDE):
        for dy in range(SIDE):
            col = ((my_x + dx) & 3) * SIDE + ((my_y + dy) & 3)
            one_out[dx][dy] = col_acc[col, :half, :].astype(jnp.bfloat16)
            two_out[dy][dx] = col_acc[col, half:, :].astype(jnp.bfloat16)


def pair_products(first, slots, own, rows, cols_one, cols_two, tiles):
    block, width = own.shape
    subs = rows.shape[0]
    rank = 128
    caps = 8
    half = block // 2
    anywhere = pl.BlockSpec(memory_space=pl.ANY)
    vmem = pl.BlockSpec(memory_space=pltpu.VMEM)
    sums = jax.ShapeDtypeStruct((SIDE, half, rank), jnp.bfloat16)
    out_shape = [
        jax.ShapeDtypeStruct((block, rank), jnp.float32),
        jax.ShapeDtypeStruct((subs, block, rank), jnp.bfloat16),
    ] + [sums] * (2 * SIDE)
    out_specs = [vmem] * len(out_shape)
    args = [slots, own, rows, *cols_one, *cols_two]
    in_specs = [pl.BlockSpec(memory_space=pltpu.SMEM), vmem] + [anywhere] * (1 + 2 * NEAR)
    if first:
        out_shape.append(jax.ShapeDtypeStruct((caps + 1, block, block), jnp.bfloat16))
        out_specs.append(anywhere)
    else:
        args.append(tiles)
        in_specs.append(anywhere)
    flops = 2 * (caps + 1) * block * block * (width + rank)
    return pl.pallas_call(
        functools.partial(pairs_kernel, first),
        out_shape=out_shape,
        in_specs=in_specs,
        out_specs=out_specs,
        scratch_shapes=[
            pltpu.VMEM((2, block, width), jnp.bfloat16),
            pltpu.VMEM((2, block, width), jnp.bfloat16),
            pltpu.VMEM((2, block, block), jnp.bfloat16),
            pltpu.VMEM((subs, block, rank), jnp.float32),
            pltpu.VMEM((SIDE * SIDE, block, rank), jnp.float32),
            pltpu.SemaphoreType.DMA((2, 4)),
            pltpu.SemaphoreType.DMA((2,)),
        ],
        compiler_params=pltpu.CompilerParams(vmem_limit_bytes=36 * 1024 * 1024),
        cost_estimate=pl.CostEstimate(flops=flops, bytes_accessed=20_000_000, transcendentals=0),
    )(*args)


def local(embeddings, subspace, pair_slots, pair_count):
    normed = normalize(embeddings)
    block = normed.shape[0]
    shards = lax.axis_size("shard")
    subs = lax.axis_size("sub")
    here = jnp.stack([pair_count.reshape(()), lax.axis_index("shard").astype(jnp.int32)])
    slots = jnp.concatenate([pair_slots.reshape(-1, 2), here[None]])
    current = subspace
    tiles = None
    for iteration in range(ITERS):
        first = iteration == 0
        basis = current.astype(jnp.bfloat16)
        own = jnp.concatenate([normed, basis], axis=1) if first else basis
        rows = lax.all_gather(own, "sub", axis=0)
        cols_one, cols_two = gather_cols(own)
        own_sum, row_sums, *others = pair_products(first, slots, own, rows, cols_one, cols_two, tiles)
        if first:
            tiles = others.pop()
        row_back = lax.psum_scatter(row_sums, "sub", scatter_dimension=0, tiled=True)
        col_back = scatter_cols(others[:SIDE], others[SIDE:])
        image = own_sum + row_back[0].astype(jnp.float32) + col_back
        local_gram = lax.dot_general(
            image,
            image,
            (((0,), (0,)), ((), ())),
            precision=lax.Precision.HIGHEST,
            preferred_element_type=jnp.float32,
        )
        gram = sum_everywhere(local_gram) / (block * shards * subs)
        factor = jnp.linalg.cholesky(gram)
        current = jax.scipy.linalg.solve_triangular(factor, image.T, lower=True).T
    return current


def solution(mesh):
    in_specs = (
        P(("shard", "sub"), None),
        P(("shard", "sub"), None),
        P("shard", "sub", None, None),
        P("shard", "sub"),
    )
    out_specs = P(("shard", "sub"), None)
    return jax.shard_map(local, mesh=mesh, in_specs=in_specs, out_specs=out_specs, check_vma=False)
```

```python
import functools
import math

import jax
import jax.numpy as jnp
from jax import lax
from jax.experimental import pallas as pl
from jax.experimental.pallas import tpu as pltpu
from jax.sharding import PartitionSpec as P

ITERS = 2
SIDE = 4
VMEM_MIB = 58

sharpness = 10.0


def prepare_kernel(embeddings, subspace, own, one, two):
    values = embeddings[...].astype(jnp.float32)
    feat = values.shape[-1]
    scale = lax.rsqrt(jnp.mean(values * values, axis=-1, keepdims=True) + 1e-06) / math.sqrt(feat)
    own[:, :feat] = (values * scale).astype(jnp.bfloat16)
    own[:, feat:] = subspace[...].astype(jnp.bfloat16)
    half = one.shape[0]
    one[...] = own[:half, :]
    two[...] = own[half:, :]


def prepare(embeddings, subspace):
    block, feat = embeddings.shape
    width = feat + subspace.shape[1]
    half = jax.ShapeDtypeStruct((block // 2, width), jnp.bfloat16)
    return pl.pallas_call(
        prepare_kernel,
        out_shape=[jax.ShapeDtypeStruct((block, width), jnp.bfloat16), half, half],
        compiler_params=pltpu.CompilerParams(vmem_limit_bytes=8 * 1024 * 1024),
    )(embeddings, subspace)


def move_x(array, step):
    pairs = [(x * SIDE + y, (x + step) % SIDE * SIDE + y) for x in range(SIDE) for y in range(SIDE)]
    return lax.ppermute(array, "shard", pairs)


def move_y(array, step):
    pairs = [(x * SIDE + y, x * SIDE + (y + step) % SIDE) for x in range(SIDE) for y in range(SIDE)]
    return lax.ppermute(array, "shard", pairs)


def move_z(array, step):
    pairs = [(z * 2 + c, (z + step) % SIDE * 2 + c) for z in range(SIDE) for c in range(2)]
    return lax.ppermute(array, "sub", pairs)


def swap_core(array):
    return lax.ppermute(array, "sub", [(z * 2 + c, z * 2 + 1 - c) for z in range(SIDE) for c in range(2)])


def total(*arrays):
    out = arrays[0].astype(jnp.float32)
    for array in arrays[1:]:
        out = out + array.astype(jnp.float32)
    return out


def gather_stack(move, array):
    return jnp.stack([array, move(array, 1), move(array, 2), move(array, 3)])


def gather_ring(move, stack):
    ahead, back = move(stack, 1), move(stack, 3)
    return [stack, ahead, back, move(ahead[:2], 1), move(back[2:], 3)]


def gather_cols(one, two):
    return gather_ring(move_x, gather_stack(move_y, one)), gather_ring(move_y, gather_stack(move_x, two))


def scatter_ring(move, parts):
    near, one, three, far_low, far_high = parts
    far_ahead, far_back = move(far_low, 1), move(far_high, 3)
    empty = jnp.zeros_like(far_ahead)
    ahead = total(one, jnp.concatenate([far_ahead, empty])).astype(jnp.bfloat16)
    back = total(three, jnp.concatenate([empty, far_back])).astype(jnp.bfloat16)
    return total(near, move(ahead, 1), move(back, 3)).astype(jnp.bfloat16)


def scatter_direct(move, stack):
    return total(stack[0], *[move(stack[d], d) for d in (1, 2, 3)])


def scatter_all(same, other, one, two):
    one, two = scatter_ring(move_x, one), scatter_ring(move_y, two)
    both = total(same, swap_core(other)).astype(jnp.bfloat16)
    both, one, two = lax.optimization_barrier((both, one, two))
    rows = scatter_direct(move_z, both)
    cols = jnp.concatenate([scatter_direct(move_y, one), scatter_direct(move_x, two)])
    return rows + cols


def sum_everywhere(gram):
    gram = gram + swap_core(gram)
    for move in (move_z, move_y):
        gram = gram + move(gram, 1) + move(gram, 2) + move(gram, 3)
    return [gram, move_x(gram, 1), move_x(gram, 2), move_x(gram, 3)]


LANES = 8


def inverse_factor(gram):
    rank = gram.shape[0]
    full = (LANES, rank)
    lane = lax.broadcasted_iota(jnp.int32, full, 1)
    line = lax.broadcasted_iota(jnp.int32, full, 0)
    rows = [gram[lo : lo + LANES, :] for lo in range(0, rank, LANES)]
    out = []
    for p in range(len(rows)):
        lo = p * LANES
        inside = (lane >= lo) & (lane < lo + LANES)
        cols = [jnp.broadcast_to(rows[p][:, lo + s : lo + s + 1], full) for s in range(LANES)]
        pivot = [[jnp.broadcast_to(cols[s][i : i + 1, :], full) for s in range(i + 1)] for i in range(LANES)]
        start = jnp.where(inside, jnp.where(lane == line + lo, 1.0, 0.0), rows[p])
        lines = [jnp.broadcast_to(start[i : i + 1, :], full) for i in range(LANES)]
        lower = [[None] * LANES for _ in range(LANES)]
        scale = [None] * LANES
        done = jnp.zeros(full, jnp.float32)
        for s in range(LANES):
            scale[s] = 1.0 / pivot[s][s]
            done = jnp.where(line == s, lines[s] * lax.rsqrt(pivot[s][s]), done)
            for i in range(s + 1, LANES):
                lower[i][s] = pivot[i][s] * scale[s]
            for i in range(s + 1, LANES):
                for j in range(s + 1, i + 1):
                    pivot[i][j] = pivot[i][j] - lower[i][s] * pivot[j][s]
                lines[i] = lines[i] - lower[i][s] * lines[s]
        out.append(jnp.where(lane <= line + lo, done, 0.0))
        lines = [lines[s] * scale[s] for s in range(LANES)]
        for s in range(LANES - 1, 0, -1):
            for i in range(s):
                lines[i] = lines[i] - lower[s][i] * lines[s]
        for h in range(p + 1, len(rows)):
            old = rows[h]
            new = jnp.where(inside, 0.0, old)
            for s in range(LANES):
                new = new - jnp.broadcast_to(old[:, lo + s : lo + s + 1], full) * lines[s]
            rows[h] = new
    return jnp.concatenate(out, axis=0)


def whiten_kernel(count, here, ahead, far, back, image, out, *halves):
    gram = (here[...] + ahead[...] + far[...] + back[...]) / count
    out[...] = lax.dot_general(
        image[...],
        inverse_factor(gram),
        (((1,), (1,)), ((), ())),
        precision=lax.Precision.HIGHEST,
        preferred_element_type=jnp.float32,
    ).astype(out.dtype)
    for n, half in enumerate(halves):
        half[...] = out[n * half.shape[0] : (n + 1) * half.shape[0], :]


def whiten(grams, image, count, last):
    block, rank = image.shape
    half = jax.ShapeDtypeStruct((block // 2, rank), jnp.bfloat16)
    whole = jax.ShapeDtypeStruct((block, rank), jnp.float32 if last else jnp.bfloat16)
    return pl.pallas_call(
        functools.partial(whiten_kernel, count),
        out_shape=[whole] if last else [whole, half, half],
        compiler_params=pltpu.CompilerParams(vmem_limit_bytes=8 * 1024 * 1024),
    )(*grams, image)


NEAR = 5
CAPS = 8


def pairs_kernel(first, *refs):
    refs = list(refs)

    def take(n):
        out = refs[:n]
        del refs[:n]
        return out

    slots, own_in = take(2)
    own_basis = None if first else take(1)[0]
    sources = [take(1 + 2 * NEAR) for _ in range(1 if first else 2)]
    own_out, *sum_outs = take(3 + 2 * NEAR)
    row_buf, col_buf, tile_buf, own_stage, row_acc, col_acc, row_stage, col_stage, zeros, later, in_sem, out_sem = refs

    block, width = row_buf.shape[1:]
    rank = own_out.shape[-1]
    half = block // 2
    feat = width - rank
    count, shard, sub = slots[CAPS, 0], slots[CAPS, 1], slots[CAPS + 1, 0]
    my_x, my_y = shard // SIDE, lax.rem(shard, SIDE)
    my_z, my_core = sub // 2, lax.rem(sub, 2)
    lanes = [pl.ds(0, width)] if first else [pl.ds(0, feat), pl.ds(feat, rank)]

    def picked(step, other):
        which = jnp.where(step < 2, step, jnp.where(step == 3, 2, jnp.where(other < 2, 3, 4)))
        return which, jnp.where((step == 2) & (other >= 2), other - 2, other)

    def row_copy(part, row, at):
        source = sources[part][0].at[row, :, pl.ds(0, lanes[part].size)]
        return pltpu.make_async_copy(source, row_buf.at[at, :, lanes[part]], in_sem.at[at, 3 * part])

    def half_copy(part, n, m, place, at):
        source = sources[part][1 + n * NEAR + m].at[place, :, pl.ds(0, lanes[part].size)]
        target = col_buf.at[at, pl.ds(n * half, half), lanes[part]]
        return pltpu.make_async_copy(source, target, in_sem.at[at, 3 * part + 1 + n])

    def start(j, at):
        col = slots[j, 1]
        step_x = (my_x - col // SIDE + SIDE) & 3
        step_y = (my_y - lax.rem(col, SIDE) + SIDE) & 3
        picks = picked(step_x, step_y), picked(step_y, step_x)
        for part in range(len(sources)):
            row_copy(part, slots[j, 0], at).start()
            for n, (which, place) in enumerate(picks):
                for m in range(NEAR):
                    pl.when(which == m)(half_copy(part, n, m, place, at).start)

    def finish(at):
        for part in range(len(sources)):
            row_copy(part, 0, at).wait()
            for n in range(2):
                half_copy(part, n, 0, 0, at).wait()

    def fill_tile(left, right):
        sims = lax.dot_general(
            left[:, :feat], right[:, :feat], (((1,), (1,)), ((), ())), preferred_element_type=jnp.float32
        )
        tile_buf[...] = jnp.exp(sharpness * (sims - 1.0)).astype(jnp.bfloat16)

    def send_row(row, stage):
        dz = (row // 2 - my_z + SIDE) & 3
        for n, here in enumerate((lax.rem(row, 2) == my_core, lax.rem(row, 2) != my_core)):
            pl.when(here)(pltpu.make_async_copy(stage, sum_outs[n].at[dz], out_sem.at[n]).start)

    def send_col(col, low, high):
        dx = (col // SIDE - my_x + SIDE) & 3
        dy = (lax.rem(col, SIDE) - my_y + SIDE) & 3
        for n, (stage, (which, place)) in enumerate(((low, picked(dx, dy)), (high, picked(dy, dx)))):
            for m in range(NEAR):
                at = 2 + n * NEAR + m
                pl.when(which == m)(pltpu.make_async_copy(stage, sum_outs[at].at[place], out_sem.at[at]).start)

    start(0, 0)

    later[count, 0] = 0
    later[count, 1] = 0

    @pl.loop(0, count)
    def _(i):
        j = count - 1 - i
        for n in range(2):
            later[j, n] = later[j + 1, n] | (1 << slots[j, n])

    def bit(mask, at):
        return ((mask >> at) & 1) == 1

    zeros[...] = jnp.zeros_like(zeros)

    @pl.loop(0, row_acc.shape[0])
    def _(row):
        pl.when(jnp.logical_not(bit(later[0, 0], row)))(lambda: send_row(row, zeros))

    @pl.loop(0, col_acc.shape[0])
    def _(col):
        low = zeros.at[pl.ds(0, half)]
        pl.when(jnp.logical_not(bit(later[0, 1], col)))(lambda: send_col(col, low, low))

    fill_tile(own_in, own_in)
    basis = own_in[:, feat:] if first else own_basis[...]
    own_stage[...] = jnp.dot(tile_buf[...], basis, preferred_element_type=jnp.float32)
    own_copy = pltpu.make_async_copy(own_stage, own_out, out_sem.at[2 + 2 * NEAR])
    own_copy.start()

    def pair(j, seen):
        at = lax.rem(j, 2)

        @pl.when(j + 1 < count)
        def _():
            start(j + 1, 1 - at)

        row, col = slots[j, 0], slots[j, 1]

        @pl.when(jnp.logical_not(bit(seen[0], row)))
        def _():
            row_acc[row] = jnp.zeros((block, rank), jnp.float32)

        @pl.when(jnp.logical_not(bit(seen[1], col)))
        def _():
            col_acc[col] = jnp.zeros((block, rank), jnp.float32)

        finish(at)
        fill_tile(row_buf.at[at], col_buf.at[at])
        row_acc[row] += jnp.dot(tile_buf[...], col_buf[at, :, feat:], preferred_element_type=jnp.float32)
        turned = lax.dot_general(
            row_buf[at, :, feat:],
            tile_buf[...],
            (((0,), (0,)), ((), ())),
            preferred_element_type=jnp.float32,
        )
        col_acc[col] += turned.T

        @pl.when(jnp.logical_not(bit(later[j + 1, 0], row)))
        def _():
            row_stage[row] = row_acc[row].astype(jnp.bfloat16)
            send_row(row, row_stage.at[row])

        @pl.when(jnp.logical_not(bit(later[j + 1, 1], col)))
        def _():
            col_stage[col] = col_acc[col].astype(jnp.bfloat16)
            send_col(col, col_stage.at[col, pl.ds(0, half)], col_stage.at[col, pl.ds(half, half)])

        return seen[0] | (1 << row), seen[1] | (1 << col)

    lax.fori_loop(0, count, pair, (jnp.int32(0), jnp.int32(0)))
    own_copy.wait()
    for n, out in enumerate(sum_outs):
        pltpu.make_async_copy(out, out, out_sem.at[n]).wait()


def pair_products(slots, feats, basis):
    first = basis is None
    block, width = feats[0].shape
    rank = 128
    width = width if first else 256 + rank
    half = block // 2
    hbm = pl.BlockSpec(memory_space=pltpu.HBM)
    vmem = pl.BlockSpec(memory_space=pltpu.VMEM)

    def sums(n, rows):
        return jax.ShapeDtypeStruct((n, rows, rank), jnp.bfloat16)

    out_shape = [jax.ShapeDtypeStruct((block, rank), jnp.float32), sums(SIDE, block), sums(SIDE, block)]
    out_shape += [sums(n, half) for n in (4, 4, 4, 2, 2)] * 2
    args, in_specs = [slots, feats[0]], [pl.BlockSpec(memory_space=pltpu.SMEM), vmem]
    if not first:
        args.append(basis[0])
        in_specs.append(vmem)
    for group in (feats,) if first else (feats, basis):
        args += [group[1], *group[2], *group[3]]
        in_specs += [hbm] * (1 + 2 * NEAR)
    flops = 2 * (CAPS + 1) * block * block * (width + rank)
    return pl.pallas_call(
        functools.partial(pairs_kernel, first),
        out_shape=out_shape,
        in_specs=in_specs,
        out_specs=[hbm] * len(out_shape),
        scratch_shapes=[
            pltpu.VMEM((2, block, width), jnp.bfloat16),
            pltpu.VMEM((2, block, width), jnp.bfloat16),
            pltpu.VMEM((block, block), jnp.bfloat16),
            pltpu.VMEM((block, rank), jnp.float32),
            pltpu.VMEM((2 * SIDE, block, rank), jnp.float32),
            pltpu.VMEM((SIDE * SIDE, block, rank), jnp.float32),
            pltpu.VMEM((2 * SIDE, block, rank), jnp.bfloat16),
            pltpu.VMEM((SIDE * SIDE, block, rank), jnp.bfloat16),
            pltpu.VMEM((block, rank), jnp.bfloat16),
            pltpu.SMEM((CAPS + 1, 2), jnp.int32),
            pltpu.SemaphoreType.DMA((2, 6)),
            pltpu.SemaphoreType.DMA((3 + 2 * NEAR,)),
        ],
        compiler_params=pltpu.CompilerParams(vmem_limit_bytes=VMEM_MIB * 1024 * 1024),
        cost_estimate=pl.CostEstimate(flops=flops, bytes_accessed=20_000_000, transcendentals=0),
    )(*args)


def local(embeddings, subspace, pair_slots, pair_count):
    block = embeddings.shape[0]
    shards = lax.axis_size("shard")
    subs = lax.axis_size("sub")
    place = [pair_count.reshape(()), lax.axis_index("shard"), lax.axis_index("sub"), 0]
    here = jnp.stack([jnp.int32(value) for value in place]).reshape(2, 2)
    slots = jnp.concatenate([pair_slots.reshape(-1, 2), here])
    held = prepare(embeddings, subspace)
    feats = None
    for iteration in range(ITERS):
        own, one, two = held
        rows = lax.all_gather(own, "sub", axis=0)
        found = (own, rows, *gather_cols(one, two))
        feats = found if feats is None else feats
        own_sum, same, other, *cols = pair_products(slots, feats, None if iteration == 0 else found)
        image = own_sum + scatter_all(same, other, cols[:NEAR], cols[NEAR:])
        local_gram = lax.dot_general(
            image,
            image,
            (((0,), (0,)), ((), ())),
            precision=lax.Precision.HIGHEST,
            preferred_element_type=jnp.float32,
        )
        last = iteration == ITERS - 1
        held = whiten(sum_everywhere(local_gram), image, block * shards * subs, last)
    return held[0]


def solution(mesh):
    in_specs = (
        P(("shard", "sub"), None),
        P(("shard", "sub"), None),
        P("shard", "sub", None, None),
        P("shard", "sub"),
    )
    out_specs = P(("shard", "sub"), None)
    return jax.shard_map(local, mesh=mesh, in_specs=in_specs, out_specs=out_specs, check_vma=False)
```

```python
import functools
import math

import jax
import jax.numpy as jnp
from jax import lax
from jax.experimental import pallas as pl
from jax.experimental.pallas import tpu as pltpu
from jax.sharding import PartitionSpec as P

ITERS = 2
SIDE = 4
VMEM_MIB = 58

sharpness = 10.0


def prepare_kernel(embeddings, subspace, own, one, two):
    values = embeddings[...].astype(jnp.float32)
    feat = values.shape[-1]
    scale = lax.rsqrt(jnp.mean(values * values, axis=-1, keepdims=True) + 1e-06) / math.sqrt(feat)
    own[:, :feat] = (values * scale).astype(jnp.bfloat16)
    own[:, feat:] = subspace[...].astype(jnp.bfloat16)
    half = one.shape[0]
    one[...] = own[:half, :]
    two[...] = own[half:, :]


def prepare(embeddings, subspace):
    block, feat = embeddings.shape
    width = feat + subspace.shape[1]
    half = jax.ShapeDtypeStruct((block // 2, width), jnp.bfloat16)
    return pl.pallas_call(
        prepare_kernel,
        out_shape=[jax.ShapeDtypeStruct((block, width), jnp.bfloat16), half, half],
        compiler_params=pltpu.CompilerParams(vmem_limit_bytes=8 * 1024 * 1024),
    )(embeddings, subspace)


def move_x(array, step):
    pairs = [(x * SIDE + y, (x + step) % SIDE * SIDE + y) for x in range(SIDE) for y in range(SIDE)]
    return lax.ppermute(array, "shard", pairs)


def move_y(array, step):
    pairs = [(x * SIDE + y, x * SIDE + (y + step) % SIDE) for x in range(SIDE) for y in range(SIDE)]
    return lax.ppermute(array, "shard", pairs)


def move_z(array, step):
    pairs = [(z * 2 + c, (z + step) % SIDE * 2 + c) for z in range(SIDE) for c in range(2)]
    return lax.ppermute(array, "sub", pairs)


def swap_core(array):
    return lax.ppermute(array, "sub", [(z * 2 + c, z * 2 + 1 - c) for z in range(SIDE) for c in range(2)])


def total(*arrays):
    out = arrays[0].astype(jnp.float32)
    for array in arrays[1:]:
        out = out + array.astype(jnp.float32)
    return out


def gather_stack(move, array):
    return jnp.stack([array, move(array, 1), move(array, 2), move(array, 3)])


def gather_ring(move, stack):
    ahead, back = move(stack, 1), move(stack, 3)
    return [stack, ahead, back, move(ahead[:2], 1), move(back[2:], 3)]


def gather_near(move, array):
    half = array.shape[0] // 2
    ahead, back = move(array, 1), move(array, 3)
    far = jnp.concatenate([move(ahead[:half], 1), move(back[half:], 3)])
    return jnp.stack([array, ahead, far, back])


def gather_cols(one, two, wide):
    stack = gather_near if wide else gather_stack
    return gather_ring(move_x, stack(move_y, one)), gather_ring(move_y, stack(move_x, two))


def scatter_far(move, parts):
    near, one, three, far_low, far_high = parts
    far = jnp.concatenate([far_low, far_high])
    return total(near, move(one, 1), move(three, 3), move(far, 2)).astype(jnp.bfloat16)


def scatter_direct(move, stack):
    return total(stack[0], *[move(stack[d], d) for d in (1, 2, 3)])


def scatter_cols(one, two):
    one, two = scatter_far(move_x, one), scatter_far(move_y, two)
    return jnp.concatenate([scatter_direct(move_y, one), scatter_direct(move_x, two)])


def sum_everywhere(gram):
    gram = gram + swap_core(gram)
    for move in (move_z, move_y):
        gram = gram + move(gram, 1) + move(gram, 2) + move(gram, 3)
    return [gram, move_x(gram, 1), move_x(gram, 2), move_x(gram, 3)]


LANES = 8


def inverse_factor(gram):
    rank = gram.shape[0]
    full = (LANES, rank)
    lane = lax.broadcasted_iota(jnp.int32, full, 1)
    line = lax.broadcasted_iota(jnp.int32, full, 0)
    rows = [gram[lo : lo + LANES, :] for lo in range(0, rank, LANES)]
    out = []
    for p in range(len(rows)):
        lo = p * LANES
        inside = (lane >= lo) & (lane < lo + LANES)
        cols = [jnp.broadcast_to(rows[p][:, lo + s : lo + s + 1], full) for s in range(LANES)]
        pivot = [[jnp.broadcast_to(cols[s][i : i + 1, :], full) for s in range(i + 1)] for i in range(LANES)]
        start = jnp.where(inside, jnp.where(lane == line + lo, 1.0, 0.0), rows[p])
        lines = [jnp.broadcast_to(start[i : i + 1, :], full) for i in range(LANES)]
        lower = [[None] * LANES for _ in range(LANES)]
        scale = [None] * LANES
        done = jnp.zeros(full, jnp.float32)
        for s in range(LANES):
            scale[s] = 1.0 / pivot[s][s]
            done = jnp.where(line == s, lines[s] * lax.rsqrt(pivot[s][s]), done)
            for i in range(s + 1, LANES):
                lower[i][s] = pivot[i][s] * scale[s]
            for i in range(s + 1, LANES):
                for j in range(s + 1, i + 1):
                    pivot[i][j] = pivot[i][j] - lower[i][s] * pivot[j][s]
                lines[i] = lines[i] - lower[i][s] * lines[s]
        out.append(jnp.where(lane <= line + lo, done, 0.0))
        lines = [lines[s] * scale[s] for s in range(LANES)]
        for s in range(LANES - 1, 0, -1):
            for i in range(s):
                lines[i] = lines[i] - lower[s][i] * lines[s]
        for h in range(p + 1, len(rows)):
            old = rows[h]
            new = jnp.where(inside, 0.0, old)
            for s in range(LANES):
                new = new - jnp.broadcast_to(old[:, lo + s : lo + s + 1], full) * lines[s]
            rows[h] = new
    return jnp.concatenate(out, axis=0)


def whiten_kernel(count, here, ahead, far, back, image, out, *halves):
    gram = (here[...] + ahead[...] + far[...] + back[...]) / count
    out[...] = lax.dot_general(
        image[...],
        inverse_factor(gram),
        (((1,), (1,)), ((), ())),
        precision=lax.Precision.HIGHEST,
        preferred_element_type=jnp.float32,
    ).astype(out.dtype)
    for n, half in enumerate(halves):
        half[...] = out[n * half.shape[0] : (n + 1) * half.shape[0], :]


def whiten(grams, image, count, last):
    block, rank = image.shape
    half = jax.ShapeDtypeStruct((block // 2, rank), jnp.bfloat16)
    whole = jax.ShapeDtypeStruct((block, rank), jnp.float32 if last else jnp.bfloat16)
    return pl.pallas_call(
        functools.partial(whiten_kernel, count),
        out_shape=[whole] if last else [whole, half, half],
        compiler_params=pltpu.CompilerParams(vmem_limit_bytes=8 * 1024 * 1024),
    )(*grams, image)


NEAR = 5
CAPS = 8


def kernel_tile(left, right):
    sims = lax.dot_general(left, right, (((1,), (1,)), ((), ())), preferred_element_type=jnp.float32)
    return jnp.exp(sharpness * (sims - 1.0)).astype(jnp.bfloat16)


def own_kernel(feats, basis, out):
    rank = out.shape[-1]
    feat = feats.shape[-1] - rank
    tile = kernel_tile(feats[:, :feat], feats[:, :feat])
    out[...] = jnp.dot(tile, basis[:, basis.shape[-1] - rank :], preferred_element_type=jnp.float32)


def own_product(feats, basis):
    block, width = feats.shape
    rank = 128
    return pl.pallas_call(
        own_kernel,
        out_shape=jax.ShapeDtypeStruct((block, rank), jnp.float32),
        compiler_params=pltpu.CompilerParams(vmem_limit_bytes=12 * 1024 * 1024),
        cost_estimate=pl.CostEstimate(flops=2 * block * block * width, bytes_accessed=1_500_000, transcendentals=0),
    )(feats, basis)


def pairs_kernel(first, *refs):
    refs = list(refs)

    def take(n):
        out = refs[:n]
        del refs[:n]
        return out

    (slots,) = take(1)
    sources = [take(1 + 2 * NEAR) for _ in range(1 if first else 2)]
    sum_outs = take(1 + 2 * NEAR)
    row_buf, col_buf, tile_buf, row_acc, col_acc, row_stage, col_stage, zeros, later, in_sem, out_sem = refs

    block, width = row_buf.shape[1:]
    rank = row_acc.shape[-1]
    half = block // 2
    feat = width - rank
    count, shard = slots[CAPS, 0], slots[CAPS, 1]
    my_x, my_y = shard // SIDE, lax.rem(shard, SIDE)
    lanes = [pl.ds(0, width)] if first else [pl.ds(0, feat), pl.ds(feat, rank)]

    def picked(step, other):
        which = jnp.where(step < 2, step, jnp.where(step == 3, 2, jnp.where(other < 2, 3, 4)))
        return which, jnp.where((step == 2) & (other >= 2), other - 2, other)

    def row_copy(part, row, at):
        source = sources[part][0].at[row, :, pl.ds(0, lanes[part].size)]
        return pltpu.make_async_copy(source, row_buf.at[at, :, lanes[part]], in_sem.at[at, 3 * part])

    def half_copy(part, n, m, place, at):
        source = sources[part][1 + n * NEAR + m].at[place, :, pl.ds(0, lanes[part].size)]
        target = col_buf.at[at, pl.ds(n * half, half), lanes[part]]
        return pltpu.make_async_copy(source, target, in_sem.at[at, 3 * part + 1 + n])

    def start(j, at):
        col = slots[j, 1]
        step_x = (my_x - col // SIDE + SIDE) & 3
        step_y = (my_y - lax.rem(col, SIDE) + SIDE) & 3
        picks = picked(step_x, step_y), picked(step_y, step_x)
        for part in range(len(sources)):
            row_copy(part, slots[j, 0], at).start()
            for n, (which, place) in enumerate(picks):
                for m in range(NEAR):
                    pl.when(which == m)(half_copy(part, n, m, place, at).start)

    def finish(at):
        for part in range(len(sources)):
            row_copy(part, 0, at).wait()
            for n in range(2):
                half_copy(part, n, 0, 0, at).wait()

    def send_row(row, stage):
        pltpu.make_async_copy(stage, sum_outs[0].at[row], out_sem.at[0]).start()

    def send_col(col, low, high):
        dx = (col // SIDE - my_x + SIDE) & 3
        dy = (lax.rem(col, SIDE) - my_y + SIDE) & 3
        for n, (stage, (which, place)) in enumerate(((low, picked(dx, dy)), (high, picked(dy, dx)))):
            for m in range(NEAR):
                at = 1 + n * NEAR + m
                pl.when(which == m)(pltpu.make_async_copy(stage, sum_outs[at].at[place], out_sem.at[at]).start)

    start(0, 0)

    later[count, 0] = 0
    later[count, 1] = 0

    @pl.loop(0, count)
    def _(i):
        j = count - 1 - i
        for n in range(2):
            later[j, n] = later[j + 1, n] | (1 << slots[j, n])

    def bit(mask, at):
        return ((mask >> at) & 1) == 1

    zeros[...] = jnp.zeros_like(zeros)

    @pl.loop(0, row_acc.shape[0])
    def _(row):
        pl.when(jnp.logical_not(bit(later[0, 0], row)))(lambda: send_row(row, zeros))

    @pl.loop(0, col_acc.shape[0])
    def _(col):
        low = zeros.at[pl.ds(0, half)]
        pl.when(jnp.logical_not(bit(later[0, 1], col)))(lambda: send_col(col, low, low))

    def pair(j, seen):
        at = lax.rem(j, 2)

        @pl.when(j + 1 < count)
        def _():
            start(j + 1, 1 - at)

        row, col = slots[j, 0], slots[j, 1]

        @pl.when(jnp.logical_not(bit(seen[0], row)))
        def _():
            row_acc[row] = jnp.zeros((block, rank), jnp.float32)

        @pl.when(jnp.logical_not(bit(seen[1], col)))
        def _():
            col_acc[col] = jnp.zeros((block, rank), jnp.float32)

        finish(at)
        tile_buf[...] = kernel_tile(row_buf[at, :, :feat], col_buf[at, :, :feat])
        row_acc[row] += jnp.dot(tile_buf[...], col_buf[at, :, feat:], preferred_element_type=jnp.float32)
        turned = lax.dot_general(
            row_buf[at, :, feat:],
            tile_buf[...],
            (((0,), (0,)), ((), ())),
            preferred_element_type=jnp.float32,
        )
        col_acc[col] += turned.T

        @pl.when(jnp.logical_not(bit(later[j + 1, 0], row)))
        def _():
            row_stage[row] = row_acc[row].astype(jnp.bfloat16)
            send_row(row, row_stage.at[row])

        @pl.when(jnp.logical_not(bit(later[j + 1, 1], col)))
        def _():
            col_stage[col] = col_acc[col].astype(jnp.bfloat16)
            send_col(col, col_stage.at[col, pl.ds(0, half)], col_stage.at[col, pl.ds(half, half)])

        return seen[0] | (1 << row), seen[1] | (1 << col)

    lax.fori_loop(0, count, pair, (jnp.int32(0), jnp.int32(0)))
    for n, out in enumerate(sum_outs):
        pltpu.make_async_copy(out, out, out_sem.at[n]).wait()


def pair_products(slots, feats, basis):
    first = basis is None
    block, width = feats[0].shape
    rank = 128
    width = width if first else 256 + rank
    half = block // 2
    hbm = pl.BlockSpec(memory_space=pltpu.HBM)

    def sums(n, rows):
        return jax.ShapeDtypeStruct((n, rows, rank), jnp.bfloat16)

    out_shape = [sums(2 * SIDE, block)] + [sums(n, half) for n in (4, 4, 4, 2, 2)] * 2
    args, in_specs = [slots], [pl.BlockSpec(memory_space=pltpu.SMEM)]
    for group in (feats,) if first else (feats, basis):
        args += [group[1], *group[2], *group[3]]
        in_specs += [hbm] * (1 + 2 * NEAR)
    flops = 2 * (CAPS + 1) * block * block * (width + rank)
    return pl.pallas_call(
        functools.partial(pairs_kernel, first),
        out_shape=out_shape,
        in_specs=in_specs,
        out_specs=[hbm] * len(out_shape),
        scratch_shapes=[
            pltpu.VMEM((2, block, width), jnp.bfloat16),
            pltpu.VMEM((2, block, width), jnp.bfloat16),
            pltpu.VMEM((block, block), jnp.bfloat16),
            pltpu.VMEM((2 * SIDE, block, rank), jnp.float32),
            pltpu.VMEM((SIDE * SIDE, block, rank), jnp.float32),
            pltpu.VMEM((2 * SIDE, block, rank), jnp.bfloat16),
            pltpu.VMEM((SIDE * SIDE, block, rank), jnp.bfloat16),
            pltpu.VMEM((block, rank), jnp.bfloat16),
            pltpu.SMEM((CAPS + 1, 2), jnp.int32),
            pltpu.SemaphoreType.DMA((2, 6)),
            pltpu.SemaphoreType.DMA((1 + 2 * NEAR,)),
        ],
        compiler_params=pltpu.CompilerParams(vmem_limit_bytes=VMEM_MIB * 1024 * 1024),
        cost_estimate=pl.CostEstimate(flops=flops, bytes_accessed=20_000_000, transcendentals=0),
    )(*args)


def local(embeddings, subspace, pair_slots, pair_count):
    block = embeddings.shape[0]
    shards = lax.axis_size("shard")
    subs = lax.axis_size("sub")
    here = jnp.stack([pair_count.reshape(()), lax.axis_index("shard").astype(jnp.int32)])
    slots = jnp.concatenate([pair_slots.reshape(-1, 2), here[None]])
    held = prepare(embeddings, subspace)
    feats = None
    for iteration in range(ITERS):
        own, one, two = held
        rows = lax.all_gather(own, "sub", axis=0)
        found = (own, rows, *gather_cols(one, two, iteration == 0))
        feats = found if feats is None else feats
        own_sum = own_product(feats[0], own)
        row_sums, *cols = pair_products(slots, feats, None if iteration == 0 else found)
        row_back = lax.psum_scatter(row_sums, "sub", scatter_dimension=0, tiled=True)
        image = own_sum + row_back[0].astype(jnp.float32) + scatter_cols(cols[:NEAR], cols[NEAR:])
        local_gram = lax.dot_general(
            image,
            image,
            (((0,), (0,)), ((), ())),
            precision=lax.Precision.HIGHEST,
            preferred_element_type=jnp.float32,
        )
        last = iteration == ITERS - 1
        held = whiten(sum_everywhere(local_gram), image, block * shards * subs, last)
    return held[0]


def solution(mesh):
    in_specs = (
        P(("shard", "sub"), None),
        P(("shard", "sub"), None),
        P("shard", "sub", None, None),
        P("shard", "sub"),
    )
    out_specs = P(("shard", "sub"), None)
    return jax.shard_map(local, mesh=mesh, in_specs=in_specs, out_specs=out_specs, check_vma=False)
```

```python
import functools
import itertools
import math

import jax
import jax.numpy as jnp
from jax import lax
from jax.experimental import pallas as pl
from jax.experimental.pallas import tpu as pltpu
from jax.sharding import PartitionSpec as P

ITERS = 2
SIDE = 4
VMEM_MIB = 58

sharpness = 10.0


def prepare_kernel(embeddings, subspace, own, one, two):
    values = embeddings[...].astype(jnp.float32)
    feat = values.shape[-1]
    scale = lax.rsqrt(jnp.mean(values * values, axis=-1, keepdims=True) + 1e-06) / math.sqrt(feat)
    own[:, :feat] = (values * scale).astype(jnp.bfloat16)
    own[:, feat:] = subspace[...].astype(jnp.bfloat16)
    half = one.shape[0]
    one[...] = own[:half, :]
    two[...] = own[half:, :]


def prepare(embeddings, subspace):
    block, feat = embeddings.shape
    width = feat + subspace.shape[1]
    half = jax.ShapeDtypeStruct((block // 2, width), jnp.bfloat16)
    return pl.pallas_call(
        prepare_kernel,
        out_shape=[jax.ShapeDtypeStruct((block, width), jnp.bfloat16), half, half],
        compiler_params=pltpu.CompilerParams(vmem_limit_bytes=8 * 1024 * 1024),
    )(embeddings, subspace)


def move_x(array, step):
    pairs = [(x * SIDE + y, (x + step) % SIDE * SIDE + y) for x in range(SIDE) for y in range(SIDE)]
    return lax.ppermute(array, "shard", pairs)


def move_y(array, step):
    pairs = [(x * SIDE + y, x * SIDE + (y + step) % SIDE) for x in range(SIDE) for y in range(SIDE)]
    return lax.ppermute(array, "shard", pairs)


def move_z(array, step):
    pairs = [(z * 2 + c, (z + step) % SIDE * 2 + c) for z in range(SIDE) for c in range(2)]
    return lax.ppermute(array, "sub", pairs)


def swap_core(array):
    return lax.ppermute(array, "sub", [(z * 2 + c, z * 2 + 1 - c) for z in range(SIDE) for c in range(2)])


def total(*arrays):
    out = arrays[0].astype(jnp.float32)
    for array in arrays[1:]:
        out = out + array.astype(jnp.float32)
    return out


def gather_stack(move, array):
    return jnp.stack([array, move(array, 1), move(array, 2), move(array, 3)])


def gather_ring(move, stack):
    ahead, back = move(stack, 1), move(stack, 3)
    return [stack, ahead, back, move(ahead[:2], 1), move(back[2:], 3)]


def gather_near(move, array):
    half = array.shape[0] // 2
    ahead, back = move(array, 1), move(array, 3)
    far = jnp.concatenate([move(ahead[:half], 1), move(back[half:], 3)])
    return jnp.stack([array, ahead, far, back])


def gather_cols(one, two, wide):
    stack = gather_near if wide else gather_stack
    return gather_ring(move_x, stack(move_y, one)), gather_ring(move_y, stack(move_x, two))


def scatter_far(move, parts):
    near, one, three, far_low, far_high = parts
    far = jnp.concatenate([far_low, far_high])
    return total(near, move(one, 1), move(three, 3), move(far, 2)).astype(jnp.bfloat16)


def scatter_direct(move, stack):
    return total(stack[0], *[move(stack[d], d) for d in (1, 2, 3)])


def scatter_cols(one, two):
    one, two = scatter_far(move_x, one), scatter_far(move_y, two)
    return jnp.concatenate([scatter_direct(move_y, one), scatter_direct(move_x, two)])


def move_in_turn(array, stage, step):
    pairs = []
    for here in itertools.product(range(SIDE), range(SIDE), range(SIDE), range(2)):
        there = list(here)
        axis = (2 + stage + here[3]) % 3
        there[axis] = (there[axis] + step) % SIDE
        pairs.append(tuple(((x * SIDE + y) * SIDE + z) * 2 + c for x, y, z, c in (here, there)))
    return lax.ppermute(array, ("shard", "sub"), pairs)


def sum_everywhere(gram):
    half = gram.shape[0] // 2
    core = lax.rem(lax.axis_index("sub"), 2)
    mine = lax.dynamic_slice_in_dim(gram, core * half, half)
    mine = mine + swap_core(lax.dynamic_slice_in_dim(gram, (1 - core) * half, half))
    for stage in range(3):
        mine = mine + move_in_turn(mine, stage, 1) + move_in_turn(mine, stage, 2) + move_in_turn(mine, stage, 3)
    theirs = swap_core(mine)
    return [jnp.where(core == 0, jnp.concatenate([mine, theirs]), jnp.concatenate([theirs, mine]))]


LANES = 8


def inverse_factor(gram):
    rank = gram.shape[0]
    full = (LANES, rank)
    lane = lax.broadcasted_iota(jnp.int32, full, 1)
    line = lax.broadcasted_iota(jnp.int32, full, 0)
    rows = [gram[lo : lo + LANES, :] for lo in range(0, rank, LANES)]
    out = []
    for p in range(len(rows)):
        lo = p * LANES
        inside = (lane >= lo) & (lane < lo + LANES)
        cols = [jnp.broadcast_to(rows[p][:, lo + s : lo + s + 1], full) for s in range(LANES)]
        pivot = [[jnp.broadcast_to(cols[s][i : i + 1, :], full) for s in range(i + 1)] for i in range(LANES)]
        start = jnp.where(inside, jnp.where(lane == line + lo, 1.0, 0.0), rows[p])
        lines = [jnp.broadcast_to(start[i : i + 1, :], full) for i in range(LANES)]
        lower = [[None] * LANES for _ in range(LANES)]
        scale = [None] * LANES
        done = jnp.zeros(full, jnp.float32)
        for s in range(LANES):
            scale[s] = 1.0 / pivot[s][s]
            done = jnp.where(line == s, lines[s] * lax.rsqrt(pivot[s][s]), done)
            for i in range(s + 1, LANES):
                lower[i][s] = pivot[i][s] * scale[s]
            for i in range(s + 1, LANES):
                for j in range(s + 1, i + 1):
                    pivot[i][j] = pivot[i][j] - lower[i][s] * pivot[j][s]
                lines[i] = lines[i] - lower[i][s] * lines[s]
        out.append(jnp.where(lane <= line + lo, done, 0.0))
        lines = [lines[s] * scale[s] for s in range(LANES)]
        for s in range(LANES - 1, 0, -1):
            for i in range(s):
                lines[i] = lines[i] - lower[s][i] * lines[s]
        for h in range(p + 1, len(rows)):
            old = rows[h]
            new = jnp.where(inside, 0.0, old)
            for s in range(LANES):
                new = new - jnp.broadcast_to(old[:, lo + s : lo + s + 1], full) * lines[s]
            rows[h] = new
    return jnp.concatenate(out, axis=0)


def whiten_kernel(count, whole, image, out, *halves):
    gram = whole[...] / count
    out[...] = lax.dot_general(
        image[...],
        inverse_factor(gram),
        (((1,), (1,)), ((), ())),
        precision=lax.Precision.HIGHEST,
        preferred_element_type=jnp.float32,
    ).astype(out.dtype)
    for n, half in enumerate(halves):
        half[...] = out[n * half.shape[0] : (n + 1) * half.shape[0], :]


def whiten(grams, image, count, last):
    block, rank = image.shape
    half = jax.ShapeDtypeStruct((block // 2, rank), jnp.bfloat16)
    whole = jax.ShapeDtypeStruct((block, rank), jnp.float32 if last else jnp.bfloat16)
    return pl.pallas_call(
        functools.partial(whiten_kernel, count),
        out_shape=[whole] if last else [whole, half, half],
        compiler_params=pltpu.CompilerParams(vmem_limit_bytes=8 * 1024 * 1024),
    )(*grams, image)


NEAR = 5
CAPS = 8


def kernel_tile(left, right):
    sims = lax.dot_general(left, right, (((1,), (1,)), ((), ())), preferred_element_type=jnp.float32)
    return jnp.exp(sharpness * (sims - 1.0)).astype(jnp.bfloat16)


def own_kernel(feats, basis, out):
    rank = out.shape[-1]
    feat = feats.shape[-1] - rank
    tile = kernel_tile(feats[:, :feat], feats[:, :feat])
    out[...] = jnp.dot(tile, basis[:, basis.shape[-1] - rank :], preferred_element_type=jnp.float32)


def own_product(feats, basis):
    block, width = feats.shape
    rank = 128
    return pl.pallas_call(
        own_kernel,
        out_shape=jax.ShapeDtypeStruct((block, rank), jnp.float32),
        compiler_params=pltpu.CompilerParams(vmem_limit_bytes=12 * 1024 * 1024),
        cost_estimate=pl.CostEstimate(flops=2 * block * block * width, bytes_accessed=1_500_000, transcendentals=0),
    )(feats, basis)


def pairs_kernel(first, *refs):
    refs = list(refs)

    def take(n):
        out = refs[:n]
        del refs[:n]
        return out

    (slots,) = take(1)
    sources = [take(1 + 2 * NEAR) for _ in range(1 if first else 2)]
    sum_outs = take(1 + 2 * NEAR)
    row_buf, col_buf, tile_buf, row_acc, col_acc, row_stage, col_stage, zeros, later, in_sem, out_sem = refs

    block, width = row_buf.shape[1:]
    rank = row_acc.shape[-1]
    half = block // 2
    feat = width - rank
    count, shard = slots[CAPS, 0], slots[CAPS, 1]
    my_x, my_y = shard // SIDE, lax.rem(shard, SIDE)
    lanes = [pl.ds(0, width)] if first else [pl.ds(0, feat), pl.ds(feat, rank)]

    def picked(step, other):
        which = jnp.where(step < 2, step, jnp.where(step == 3, 2, jnp.where(other < 2, 3, 4)))
        return which, jnp.where((step == 2) & (other >= 2), other - 2, other)

    def row_copy(part, row, at):
        source = sources[part][0].at[row, :, pl.ds(0, lanes[part].size)]
        return pltpu.make_async_copy(source, row_buf.at[at, :, lanes[part]], in_sem.at[at, 3 * part])

    def half_copy(part, n, m, place, at):
        source = sources[part][1 + n * NEAR + m].at[place, :, pl.ds(0, lanes[part].size)]
        target = col_buf.at[at, pl.ds(n * half, half), lanes[part]]
        return pltpu.make_async_copy(source, target, in_sem.at[at, 3 * part + 1 + n])

    def start(j, at):
        col = slots[j, 1]
        step_x = (my_x - col // SIDE + SIDE) & 3
        step_y = (my_y - lax.rem(col, SIDE) + SIDE) & 3
        picks = picked(step_x, step_y), picked(step_y, step_x)
        for part in range(len(sources)):
            row_copy(part, slots[j, 0], at).start()
            for n, (which, place) in enumerate(picks):
                for m in range(NEAR):
                    pl.when(which == m)(half_copy(part, n, m, place, at).start)

    def finish(at):
        for part in range(len(sources)):
            row_copy(part, 0, at).wait()
            for n in range(2):
                half_copy(part, n, 0, 0, at).wait()

    def send_row(row, stage):
        pltpu.make_async_copy(stage, sum_outs[0].at[row], out_sem.at[0]).start()

    def send_col(col, low, high):
        dx = (col // SIDE - my_x + SIDE) & 3
        dy = (lax.rem(col, SIDE) - my_y + SIDE) & 3
        for n, (stage, (which, place)) in enumerate(((low, picked(dx, dy)), (high, picked(dy, dx)))):
            for m in range(NEAR):
                at = 1 + n * NEAR + m
                pl.when(which == m)(pltpu.make_async_copy(stage, sum_outs[at].at[place], out_sem.at[at]).start)

    start(0, 0)

    later[count, 0] = 0
    later[count, 1] = 0

    @pl.loop(0, count)
    def _(i):
        j = count - 1 - i
        for n in range(2):
            later[j, n] = later[j + 1, n] | (1 << slots[j, n])

    def bit(mask, at):
        return ((mask >> at) & 1) == 1

    zeros[...] = jnp.zeros_like(zeros)

    @pl.loop(0, row_acc.shape[0])
    def _(row):
        pl.when(jnp.logical_not(bit(later[0, 0], row)))(lambda: send_row(row, zeros))

    @pl.loop(0, col_acc.shape[0])
    def _(col):
        low = zeros.at[pl.ds(0, half)]
        pl.when(jnp.logical_not(bit(later[0, 1], col)))(lambda: send_col(col, low, low))

    def pair(j, seen):
        at = lax.rem(j, 2)

        @pl.when(j + 1 < count)
        def _():
            start(j + 1, 1 - at)

        row, col = slots[j, 0], slots[j, 1]

        @pl.when(jnp.logical_not(bit(seen[0], row)))
        def _():
            row_acc[row] = jnp.zeros((block, rank), jnp.float32)

        @pl.when(jnp.logical_not(bit(seen[1], col)))
        def _():
            col_acc[col] = jnp.zeros((block, rank), jnp.float32)

        finish(at)
        tile_buf[...] = kernel_tile(row_buf[at, :, :feat], col_buf[at, :, :feat])
        row_acc[row] += jnp.dot(tile_buf[...], col_buf[at, :, feat:], preferred_element_type=jnp.float32)
        turned = lax.dot_general(
            row_buf[at, :, feat:],
            tile_buf[...],
            (((0,), (0,)), ((), ())),
            preferred_element_type=jnp.float32,
        )
        col_acc[col] += turned.T

        @pl.when(jnp.logical_not(bit(later[j + 1, 0], row)))
        def _():
            row_stage[row] = row_acc[row].astype(jnp.bfloat16)
            send_row(row, row_stage.at[row])

        @pl.when(jnp.logical_not(bit(later[j + 1, 1], col)))
        def _():
            col_stage[col] = col_acc[col].astype(jnp.bfloat16)
            send_col(col, col_stage.at[col, pl.ds(0, half)], col_stage.at[col, pl.ds(half, half)])

        return seen[0] | (1 << row), seen[1] | (1 << col)

    lax.fori_loop(0, count, pair, (jnp.int32(0), jnp.int32(0)))
    for n, out in enumerate(sum_outs):
        pltpu.make_async_copy(out, out, out_sem.at[n]).wait()


def pair_products(slots, feats, basis):
    first = basis is None
    block, width = feats[0].shape
    rank = 128
    width = width if first else 256 + rank
    half = block // 2
    hbm = pl.BlockSpec(memory_space=pltpu.HBM)

    def sums(n, rows):
        return jax.ShapeDtypeStruct((n, rows, rank), jnp.bfloat16)

    out_shape = [sums(2 * SIDE, block)] + [sums(n, half) for n in (4, 4, 4, 2, 2)] * 2
    args, in_specs = [slots], [pl.BlockSpec(memory_space=pltpu.SMEM)]
    for group in (feats,) if first else (feats, basis):
        args += [group[1], *group[2], *group[3]]
        in_specs += [hbm] * (1 + 2 * NEAR)
    flops = 2 * (CAPS + 1) * block * block * (width + rank)
    return pl.pallas_call(
        functools.partial(pairs_kernel, first),
        out_shape=out_shape,
        in_specs=in_specs,
        out_specs=[hbm] * len(out_shape),
        scratch_shapes=[
            pltpu.VMEM((2, block, width), jnp.bfloat16),
            pltpu.VMEM((2, block, width), jnp.bfloat16),
            pltpu.VMEM((block, block), jnp.bfloat16),
            pltpu.VMEM((2 * SIDE, block, rank), jnp.float32),
            pltpu.VMEM((SIDE * SIDE, block, rank), jnp.float32),
            pltpu.VMEM((2 * SIDE, block, rank), jnp.bfloat16),
            pltpu.VMEM((SIDE * SIDE, block, rank), jnp.bfloat16),
            pltpu.VMEM((block, rank), jnp.bfloat16),
            pltpu.SMEM((CAPS + 1, 2), jnp.int32),
            pltpu.SemaphoreType.DMA((2, 6)),
            pltpu.SemaphoreType.DMA((1 + 2 * NEAR,)),
        ],
        compiler_params=pltpu.CompilerParams(vmem_limit_bytes=VMEM_MIB * 1024 * 1024),
        cost_estimate=pl.CostEstimate(flops=flops, bytes_accessed=20_000_000, transcendentals=0),
    )(*args)


def local(embeddings, subspace, pair_slots, pair_count):
    block = embeddings.shape[0]
    shards = lax.axis_size("shard")
    subs = lax.axis_size("sub")
    here = jnp.stack([pair_count.reshape(()), lax.axis_index("shard").astype(jnp.int32)])
    slots = jnp.concatenate([pair_slots.reshape(-1, 2), here[None]])
    held = prepare(embeddings, subspace)
    feats = None
    for iteration in range(ITERS):
        own, one, two = held
        rows = lax.all_gather(own, "sub", axis=0)
        found = (own, rows, *gather_cols(one, two, iteration == 0))
        feats = found if feats is None else feats
        slots, own_sum = lax.optimization_barrier((slots, own_product(feats[0], own)))
        row_sums, *cols = pair_products(slots, feats, None if iteration == 0 else found)
        row_back = lax.psum_scatter(row_sums, "sub", scatter_dimension=0, tiled=True)
        image = own_sum + row_back[0].astype(jnp.float32) + scatter_cols(cols[:NEAR], cols[NEAR:])
        local_gram = lax.dot_general(
            image,
            image,
            (((0,), (0,)), ((), ())),
            precision=lax.Precision.HIGHEST,
            preferred_element_type=jnp.float32,
        )
        last = iteration == ITERS - 1
        held = whiten(sum_everywhere(local_gram), image, block * shards * subs, last)
    return held[0]


def solution(mesh):
    in_specs = (
        P(("shard", "sub"), None),
        P(("shard", "sub"), None),
        P("shard", "sub", None, None),
        P("shard", "sub"),
    )
    out_specs = P(("shard", "sub"), None)
    return jax.shard_map(local, mesh=mesh, in_specs=in_specs, out_specs=out_specs, check_vma=False)
```
